32 devices in a mesh: shell: 4 (over x, core), tile: 8 (over z, y).
Axes of the slice: x: 2, y: 2, z: 4, core: 2. Of those that a mesh axis runs over, the one named last changes fastest.
Arguments:
- sky_grad: float32 [10, 8192, 128], P(None, ('tile', 'shell')), may hold values from -6 to 6
- kernel: float32 [10, 8], replicated, may hold values from 0.05 to 1
- owner_dev: int32 [8, 8192, 1], P('shell', 'tile'), may hold values from 0 to 7; in each aligned block of 1024 rows (0 to 1023, 1024 to 2047, ..., all dimensions but the last counted through in order) at most 512 rows name the same one
- cell_index: int32 [8, 8192], P('shell', 'tile'), may hold values from 0 to 255
- level_index: int32 [8, 8192], P('shell', 'tile'), may hold values from 0 to 255
Outputs:
- shell_grad: float32 [8, 2048, 128], P('shell', 'tile')
The draws below stay inside these ranges and needn't reach their ends.
Inputs may be any that keep to these rules, and one draw needn't show every extreme that they name: `owner_dev`: among the 1024 sky blocks of one sky tile and one shell, no owner is named more than 512 times, a bound that some block reaches.
All inputs are finite; a program needn't handle non-finite values.
Results may differ from the reference program's by a relative error of at most 0.00007.
Values sent between devices are 32-bit elements; how exact they have to be, the bound alone decides.
A program may use at most 64 MiB of HBM per device.

```python
import math
import jax
import jax.numpy as jnp
import numpy as np
from jax import lax

BINS = 10
LEVELS = 256
SKY_TILE = 1024
BLK_DEV = 256
RB = 16
SHELLS = 8
SKY_BLOCKS = 8192
CAP = 512
N_TILE = 8


def touch_ends(entries, rng, least, top_value):
    shape = entries.shape
    place = [jax.random.randint(jax.random.fold_in(rng, axis), (), 0, shape[axis]) for axis in range(len(shape))]
    entries = entries.at[tuple(place)].set(least)
    longest = shape.index(max(shape))
    place[longest] = (place[longest] + 1) % shape[longest]
    return entries.at[tuple(place)].set(top_value)


def block_levels(rng, extent, cuts, low, largest):
    def one(dim, shards_of):
        draws = jax.random.uniform(jax.random.fold_in(jax.random.fold_in(rng, 6), dim), (shards_of,), jnp.float32, low / len(cuts), largest / len(cuts))
        return jnp.repeat(jnp.exp(draws), extent[dim] // shards_of).reshape((-1,) + (1,) * (len(extent) - dim - 1))

    factor_of = one(*cuts[0])
    for cut in cuts[1:]:
        factor_of = factor_of * one(*cut)
    return factor_of


def routed_block(rng, own, number, rows, count, top, reach, lean):
    sequence = jax.random.permutation(rng, count)
    heavy_load, common = load_shares(count, rows * top, reach, lean, True), load_shares(count, rows * top, reach, lean, False)
    places = jnp.arange(count)

    def named(tallies, turn):
        used = int((tallies > 0).sum())
        fixed = max(1, used // 4)
        shifted = fixed + (places - fixed + turn * (used - fixed)) % max(1, count - fixed)
        return jnp.zeros((count,), jnp.int32).at[sequence[jnp.where(places < fixed, places, shifted)]].set(jnp.asarray(tallies, jnp.int32))

    tallies = jnp.where(number % 4 == 0, named(heavy_load, number // 4), named(common, number - number // 4 - 1))
    mixed = jax.random.permutation(jax.random.fold_in(own, 3), count)
    giver, receiver = mixed[0:count // 2 * 2:2], mixed[1:count // 2 * 2:2]
    slack = jnp.minimum(tallies[giver] - 1, reach - tallies[receiver]) // 2
    slack = jnp.where((giver == sequence[0]) | (receiver == sequence[0]) | (tallies[receiver] == 0), 0, jnp.maximum(slack, 0))
    shifted = jax.random.randint(jax.random.fold_in(own, 4), (count // 2,), 0, 1 << 20) % (slack + 1)
    tallies = tallies.at[giver].add(-shifted).at[receiver].add(shifted)
    labels = jnp.searchsorted(jnp.cumsum(tallies), jnp.arange(rows * top), side="right").astype(jnp.int32)
    grid = labels.reshape(top, rows).T
    grid = grid[jax.random.permutation(jax.random.fold_in(own, 1), rows)]
    turn = jax.random.randint(jax.random.fold_in(own, 2), (rows, 1), 0, top)
    return jnp.take_along_axis(grid, (jnp.arange(top)[None, :] + turn) % top, axis=1)


def load_shares(number_of, total, reach, lean, full):
    loads = [(1 << 20) // math.isqrt(standing ** lean) + 1 for standing in range(1, number_of + 1)]
    largest = reach if full else min(reach, max(-(-total // number_of), total * loads[0] // sum(loads)))
    least = 1 if total - largest >= number_of - 1 else 0
    given, surplus = [largest] + [least] * (number_of - 1), total - largest - least * (number_of - 1)
    while surplus > 0:
        free = [i for i in range(1, number_of) if given[i] < largest] or [i for i in range(1, number_of) if given[i] < reach]
        whole, left = sum([loads[i] for i in free]), surplus
        for i in free:
            addition = min(reach - given[i], max(1, left * loads[i] // whole), surplus)
            given[i] = given[i] + addition
            surplus = surplus - addition
    return np.array(given)


def noise(key, shape, deviation, reach, cuts=(), kind=jnp.bfloat16):
    array = jax.random.normal(key, shape, jnp.float32) * deviation
    if len(cuts) > 0:
        array = block_levels(key, shape, cuts, -0.22, 0.18) * array
    return jnp.clip(array, min=-reach, max=reach).astype(kind)


def setup_inputs(seed: int = 0) -> dict:
    keys = jax.random.split(jax.random.key(seed), 6)
    sky_grad = noise(keys[0], (BINS, SKY_BLOCKS, 128), 1.0, 6.0, ((1, 32),), jnp.float32)
    kernel = jnp.clip(jnp.exp(jax.random.uniform(keys[1], (BINS, SHELLS), jnp.float32, math.log(0.05), math.log(1.0))), 0.05, 1.0)
    owner_dev_keys = jax.random.split(jax.random.fold_in(keys[2], 1), SHELLS * SKY_BLOCKS // SKY_TILE)
    owner_dev_turns = jax.random.permutation(jax.random.fold_in(keys[2], 3), SHELLS * SKY_BLOCKS // SKY_TILE)
    owner_dev = jax.vmap(lambda own, number: routed_block(jax.random.fold_in(keys[2], 2), own, number, SKY_TILE, N_TILE, 1, CAP, 2))(owner_dev_keys, owner_dev_turns).reshape((SHELLS, SKY_BLOCKS, 1))
    cell_index = touch_ends(jax.random.randint(keys[3], (SHELLS, SKY_BLOCKS), 0, BLK_DEV), jax.random.fold_in(keys[3], 1), 0, BLK_DEV - 1).astype(jnp.int32)
    level_index = touch_ends(jax.random.randint(keys[4], (SHELLS, SKY_BLOCKS), 0, LEVELS), jax.random.fold_in(keys[4], 1), 0, LEVELS - 1).astype(jnp.int32)
    return dict(sky_grad=sky_grad, kernel=kernel, owner_dev=owner_dev, cell_index=cell_index, level_index=level_index)


def reference(sky_grad, kernel, owner_dev, cell_index, level_index):
    reduced = jnp.einsum('bs,brc->src', kernel, sky_grad, precision=lax.Precision.HIGHEST)
    fraction = (level_index.astype(jnp.float32) + 0.5) / LEVELS
    destination = (owner_dev[:, :, 0] * BLK_DEV + cell_index).astype(jnp.int32)
    grid_blocks = N_TILE * BLK_DEV
    shell_ids = jnp.broadcast_to(jnp.arange(SHELLS, dtype=jnp.int32)[:, None], destination.shape)
    shell_grad = jnp.zeros((SHELLS, grid_blocks, 128), jnp.float32)
    shell_grad = shell_grad.at[shell_ids, destination].add((1.0 - fraction)[:, :, None] * reduced)
    shell_grad = shell_grad.at[shell_ids, destination + RB].add(fraction[:, :, None] * reduced, mode="drop")
    return shell_grad
```

```python
import functools
import math

import jax
import jax.numpy as jnp
from jax import lax
from jax.experimental import pallas as pl
from jax.experimental.pallas import tpu as pltpu
from jax.sharding import PartitionSpec as P

LEVELS = 256
BLK_DEV = 256
RB = 16
EXT = BLK_DEV + RB
LANES = 128
MESH = pl.DeviceIdType.MESH


def body(
    groups, near, far,
    sky_hbm, kern, index, out,
    sky, red, rows, halves, index_all, part, landed,
    load_sem, send_sem, recv_sem, index_send, index_recv, far_send, far_recv,
):
    bins, here, _ = sky.shape
    per_group = rows.shape[0]
    group = lax.axis_index("shell")
    tile = lax.axis_index("tile")
    hi = tile // near
    lo = tile % near

    def device(group_to, hi_to, lo_to):
        return {"shell": group_to, "tile": hi_to * near + lo_to}

    load = pltpu.make_async_copy(sky_hbm, sky, load_sem)
    load.start()

    barrier = pltpu.get_barrier_semaphore()
    peers = [(d, e) for d in range(groups) for e in range(near) if (d, e) != (0, 0)]
    for d, e in peers:
        pl.semaphore_signal(
            barrier, inc=1, device_id_type=MESH,
            device_id=device((group + d) % groups, hi, (lo + e) % near),
        )
    for f in range(1, far):
        pl.semaphore_signal(
            barrier, inc=1, device_id_type=MESH, device_id=device(group, (hi + f) % far, lo)
        )

    def row_copy(s, d, e):
        return pltpu.make_async_remote_copy(
            src_ref=red.at[s, d],
            dst_ref=rows.at[s, lo, pl.ds(pl.multiple_of(group * here, here), here)],
            send_sem=send_sem.at[s, d, e],
            recv_sem=recv_sem.at[s, d, e],
            device_id=device((group + d) % groups, hi, (lo + e) % near),
            device_id_type=MESH,
        )

    def index_copy(e):
        return pltpu.make_async_remote_copy(
            src_ref=index,
            dst_ref=index_all.at[lo],
            send_sem=index_send.at[e],
            recv_sem=index_recv.at[e],
            device_id=device(group, hi, (lo + e) % near),
            device_id_type=MESH,
        )

    def far_copy(s, to, slot):
        return pltpu.make_async_remote_copy(
            src_ref=part.at[s, to],
            dst_ref=landed.at[s, slot],
            send_sem=far_send.at[s, to],
            recv_sem=far_recv.at[s, slot],
            device_id=device(group, to, lo),
            device_id_type=MESH,
        )

    def reduce_bins(s, d):
        shell = ((group + d) % groups) * per_group + s
        total = kern[0, shell] * sky[0]
        for b in range(1, bins):
            total = total + kern[b, shell] * sky[b]
        return total

    index_all[lo] = index[...]
    load.wait()
    order = sorted(range(groups), key=lambda d: (d == 0, abs(d - groups // 2)))
    for s in range(per_group):
        for n, d in enumerate(order):
            red[s, d] = reduce_bins(s, d)
            if s == 0 and n == 0:
                pl.semaphore_wait(barrier, len(peers) + far - 1)
                for e in range(1, near):
                    index_copy(e).start()
            for e in reversed(range(near)):
                if (d, e) != (0, 0):
                    row_copy(s, d, e).start()
        rows[s, lo, pl.ds(pl.multiple_of(group * here, here), here)] = red[s, 0]

    for e in range(1, near):
        index_copy(e).wait()

    low_half = hi < far // 2
    flipped = jnp.where(low_half, hi, far - 1 - hi)
    above = far - 1 - flipped
    for s in range(per_group):
        for d, e in peers:
            row_copy(s, d, e).wait_recv()
        for n in range(near):
            whole = rows[s, n]
            top = whole.astype(jnp.bfloat16)
            halves[n, :, :LANES] = top
            halves[n, :, LANES:] = (whole - top.astype(jnp.float32)).astype(jnp.bfloat16)

        @pl.loop(0, far)
        def _(k):
            to = jnp.where(k < above, far - 1 - k, k - above)
            to = jnp.where(low_half, to, far - 1 - to)
            first = (to * near + lo) * BLK_DEV - RB
            total = jnp.zeros((2 * EXT, 2 * LANES), jnp.float32)
            for n in range(near):
                place = index_all[n, s : s + 1, :] - first
                level = index_all[n, per_group + s : per_group + s + 1, :].astype(jnp.float32)
                level = jnp.broadcast_to(level * (1.0 / LEVELS), (EXT, level.shape[1]))
                hit = lax.broadcasted_iota(jnp.int32, (EXT, place.shape[1]), 0) == place
                ones = jnp.where(hit, 1.0, 0.0).astype(jnp.bfloat16)
                levels = jnp.where(hit, level, 0.0).astype(jnp.bfloat16)
                total = total + jnp.dot(
                    jnp.concatenate([ones, levels], axis=0), halves[n],
                    preferred_element_type=jnp.float32,
                )
            total = total[:, :LANES] + total[:, LANES:]
            landing = total[:EXT]
            shifted = total[EXT:] + landing * (0.5 / LEVELS)
            part[s, to] = landing[RB:] - shifted[RB:] + shifted[:BLK_DEV]

            @pl.when(to != hi)
            def _():
                far_copy(s, to, hi).start()

    for s in range(per_group):
        total = part[s, hi]
        for f in range(1, far):
            source = (hi + f) % far
            far_copy(s, source, source).wait_recv()
            total = total + landed[s, source]
        out[s] = total

    for s in range(per_group):
        for d, e in peers:
            row_copy(s, d, e).wait_send()
        for f in range(1, far):
            to = (hi + f) % far
            far_copy(s, to, to).wait_send()


def shards(near, sky_grad, kernel, owner_dev, cell_index, level_index):
    groups, tiles = lax.axis_size("shell"), lax.axis_size("tile")
    far = tiles // near
    bins, here, lanes = sky_grad.shape
    per_group, tile_rows = cell_index.shape
    index = jnp.concatenate([owner_dev[:, :, 0] * BLK_DEV + cell_index, level_index], axis=0)
    f32 = jnp.float32
    vmem = pl.BlockSpec(memory_space=pltpu.VMEM)
    return pl.pallas_call(
        functools.partial(body, groups, near, far),
        out_shape=jax.ShapeDtypeStruct((per_group, BLK_DEV, lanes), f32),
        in_specs=[
            pl.BlockSpec(memory_space=pl.ANY),
            pl.BlockSpec(memory_space=pltpu.SMEM),
            vmem,
        ],
        out_specs=vmem,
        scratch_shapes=[
            pltpu.VMEM((bins, here, lanes), f32),
            pltpu.VMEM((per_group, groups, here, lanes), f32),
            pltpu.VMEM((per_group, near, tile_rows, lanes), f32),
            pltpu.VMEM((near, tile_rows, 2 * lanes), jnp.bfloat16),
            pltpu.VMEM((near, 2 * per_group, tile_rows), jnp.int32),
            pltpu.VMEM((per_group, far, BLK_DEV, lanes), f32),
            pltpu.VMEM((per_group, far, BLK_DEV, lanes), f32),
            pltpu.SemaphoreType.DMA,
            pltpu.SemaphoreType.DMA((per_group, groups, near)),
            pltpu.SemaphoreType.DMA((per_group, groups, near)),
            pltpu.SemaphoreType.DMA((near,)),
            pltpu.SemaphoreType.DMA((near,)),
            pltpu.SemaphoreType.DMA((per_group, far)),
            pltpu.SemaphoreType.DMA((per_group, far)),
        ],
        compiler_params=pltpu.CompilerParams(
            collective_id=0, has_side_effects=True, vmem_limit_bytes=40 << 20
        ),
    )(sky_grad, kernel, index)


def solution(mesh):
    near = 1 << (int(math.log2(mesh.shape["tile"])) // 2)
    return jax.shard_map(
        functools.partial(shards, near),
        mesh=mesh,
        in_specs=(
            P(None, ("tile", "shell"), None),
            P(),
            P("shell", "tile", None),
            P("shell", "tile"),
            P("shell", "tile"),
        ),
        out_specs=P("shell", "tile", None),
        check_vma=False,
    )
```

```python
import functools
import math

import jax
import jax.numpy as jnp
from jax import lax
from jax.experimental import pallas as pl
from jax.experimental.pallas import tpu as pltpu
from jax.sharding import PartitionSpec as P

LEVELS = 256
BLK_DEV = 256
RB = 16
EXT = BLK_DEV + RB
LANES = 128
MESH = pl.DeviceIdType.MESH


def body(
    groups, near, far,
    sky_hbm, kern, owner_hbm, cell_hbm, level_hbm, out,
    sky, owner, cell, level_in, index, red, rows, halves, index_all, part, landed, relay,
    load_sem, send_sem, recv_sem, index_send, index_recv, far_send, far_recv, relay_recv,
):
    bins, here, _ = sky.shape
    per_group = rows.shape[0]
    group = lax.axis_index("shell")
    tile = lax.axis_index("tile")
    hi = tile // near
    lo = tile % near

    low_half = hi < far // 2
    flipped = jnp.where(low_half, hi, far - 1 - hi)
    relayed = far >= 4
    visits = []
    for h in range(max(1, far // 2)):
        others = sorted((t for t in range(far) if t != h), key=lambda t: (-abs(t - h), t))
        if relayed and h == 1:
            others = [t for t in others if t != far - 1] + [h, far - 1]
        else:
            others = others + [h]
        visits.append(others)

    def visit(k):
        to = jnp.int32(0)
        for h, others in enumerate(visits):
            for n, t in enumerate(others):
                to = jnp.where((flipped == h) & (k == n), t, to)
        return jnp.where(low_half, to, far - 1 - to)

    def device(group_to, hi_to, lo_to):
        return {"shell": group_to, "tile": hi_to * near + lo_to}

    loads = [
        pltpu.make_async_copy(source, target, load_sem.at[n])
        for n, (source, target) in enumerate(
            [(sky_hbm, sky), (owner_hbm, owner), (cell_hbm, cell), (level_hbm, level_in)]
        )
    ]
    for load in loads:
        load.start()

    barrier = pltpu.get_barrier_semaphore()
    peers = [(d, e) for d in range(groups) for e in range(near) if (d, e) != (0, 0)]
    for d, e in peers:
        pl.semaphore_signal(
            barrier, inc=1, device_id_type=MESH,
            device_id=device((group + d) % groups, hi, (lo + e) % near),
        )
    for f in range(1, far):
        pl.semaphore_signal(
            barrier, inc=1, device_id_type=MESH, device_id=device(group, (hi + f) % far, lo)
        )

    def row_copy(s, d, e):
        return pltpu.make_async_remote_copy(
            src_ref=red.at[s, d],
            dst_ref=rows.at[s, lo, pl.ds(pl.multiple_of(group * here, here), here)],
            send_sem=send_sem.at[s, d, e],
            recv_sem=recv_sem.at[s, d, e],
            device_id=device((group + d) % groups, hi, (lo + e) % near),
            device_id_type=MESH,
        )

    def index_copy(e):
        return pltpu.make_async_remote_copy(
            src_ref=index,
            dst_ref=index_all.at[lo],
            send_sem=index_send.at[e],
            recv_sem=index_recv.at[e],
            device_id=device(group, hi, (lo + e) % near),
            device_id_type=MESH,
        )

    def far_copy(s, to, slot):
        return pltpu.make_async_remote_copy(
            src_ref=part.at[s, to],
            dst_ref=landed.at[s, slot],
            send_sem=far_send.at[s, to],
            recv_sem=far_recv.at[s, slot],
            device_id=device(group, to, lo),
            device_id_type=MESH,
        )

    def relay_copy(s, to):
        return pltpu.make_async_remote_copy(
            src_ref=part.at[s, to],
            dst_ref=relay.at[s],
            send_sem=far_send.at[s, to],
            recv_sem=relay_recv.at[s],
            device_id=device(group, jnp.where(low_half, 1, far - 2), lo),
            device_id_type=MESH,
        )

    def reduce_bins(s, d):
        shell = ((group + d) % groups) * per_group + s
        total = kern[shell, 0] * sky[0]
        for b in range(1, bins):
            total = total + kern[shell, b] * sky[b]
        return total

    for load in loads[1:]:
        load.wait()
    for s in range(per_group):
        index[s : s + 1, :] = owner[s] * BLK_DEV + cell[s : s + 1, :]
        index[per_group + s : per_group + s + 1, :] = level_in[s : s + 1, :]
    index_all[lo] = index[...]
    loads[0].wait()
    order = sorted(range(groups), key=lambda d: (d == 0, abs(d - groups // 2)))
    for s in range(per_group):
        for n, d in enumerate(order):
            red[s, d] = reduce_bins(s, d)
            if s == 0 and n == 0:
                pl.semaphore_wait(barrier, len(peers) + far - 1)
                for e in range(1, near):
                    index_copy(e).start()
            for e in reversed(range(near)):
                if (d, e) != (0, 0):
                    row_copy(s, d, e).start()
        rows[s, lo, pl.ds(pl.multiple_of(group * here, here), here)] = red[s, 0]

    for e in range(1, near):
        index_copy(e).wait()

    for s in range(per_group):
        for d, e in peers:
            row_copy(s, d, e).wait_recv()
        for n in range(near):
            whole = rows[s, n]
            top = whole.astype(jnp.bfloat16)
            halves[n, :, :LANES] = top
            halves[n, :, LANES:] = (whole - top.astype(jnp.float32)).astype(jnp.bfloat16)

        @pl.loop(0, far)
        def _(k):
            to = visit(k)
            first = (to * near + lo) * BLK_DEV - RB
            total = jnp.zeros((2 * EXT, 2 * LANES), jnp.float32)
            for n in range(near):
                place = index_all[n, s : s + 1, :] - first
                level = index_all[n, per_group + s : per_group + s + 1, :].astype(jnp.float32)
                level = jnp.broadcast_to(level * (1.0 / LEVELS), (EXT, level.shape[1]))
                hit = lax.broadcasted_iota(jnp.int32, (EXT, place.shape[1]), 0) == place
                ones = jnp.where(hit, 1.0, 0.0).astype(jnp.bfloat16)
                levels = jnp.where(hit, level, 0.0).astype(jnp.bfloat16)
                total = total + jnp.dot(
                    jnp.concatenate([ones, levels], axis=0), halves[n],
                    preferred_element_type=jnp.float32,
                )
            total = total[:, :LANES] + total[:, LANES:]
            landing = total[:EXT]
            shifted = total[EXT:] + landing * (0.5 / LEVELS)
            part[s, to] = landing[RB:] - shifted[RB:] + shifted[:BLK_DEV]

            ends = (to == jnp.where(low_half, far - 1, 0)) & relayed

            @pl.when(ends & (flipped == 1))
            def _():
                relay_copy(s, to).wait_recv()
                part[s, to] += relay[s]

            @pl.when(ends & (flipped == 0))
            def _():
                relay_copy(s, to).start()

            @pl.when((to != hi) & jnp.logical_not(ends & (flipped == 0)))
            def _():
                far_copy(s, to, hi).start()

    for s in range(per_group):
        out[s] = part[s, hi]
        for f in range(1, far):
            source = (hi + f) % far

            @pl.when(jnp.logical_not(relayed & (jnp.abs(source - hi) == far - 1)))
            def _():
                far_copy(s, source, source).wait_recv()
                out[s] += landed[s, source]

    for s in range(per_group):
        for d, e in peers:
            row_copy(s, d, e).wait_send()
        for f in range(1, far):
            to = (hi + f) % far
            far_copy(s, to, to).wait_send()


def shards(near, sky_grad, kernel, owner_dev, cell_index, level_index):
    groups, tiles = lax.axis_size("shell"), lax.axis_size("tile")
    far = tiles // near
    bins, here, lanes = sky_grad.shape
    per_group, tile_rows = cell_index.shape
    f32 = jnp.float32
    hbm = pl.BlockSpec(memory_space=pl.ANY)
    return pl.pallas_call(
        functools.partial(body, groups, near, far),
        out_shape=jax.ShapeDtypeStruct((per_group, BLK_DEV, lanes), f32),
        in_specs=[hbm, pl.BlockSpec(memory_space=pltpu.SMEM), hbm, hbm, hbm],
        out_specs=pl.BlockSpec(memory_space=pltpu.VMEM),
        scratch_shapes=[
            pltpu.VMEM((bins, here, lanes), f32),
            pltpu.VMEM((per_group, 1, tile_rows), jnp.int32),
            pltpu.VMEM((per_group, tile_rows), jnp.int32),
            pltpu.VMEM((per_group, tile_rows), jnp.int32),
            pltpu.VMEM((2 * per_group, tile_rows), jnp.int32),
            pltpu.VMEM((per_group, groups, here, lanes), f32),
            pltpu.VMEM((per_group, near, tile_rows, lanes), f32),
            pltpu.VMEM((near, tile_rows, 2 * lanes), jnp.bfloat16),
            pltpu.VMEM((near, 2 * per_group, tile_rows), jnp.int32),
            pltpu.VMEM((per_group, far, BLK_DEV, lanes), f32),
            pltpu.VMEM((per_group, far, BLK_DEV, lanes), f32),
            pltpu.VMEM((per_group, BLK_DEV, lanes), f32),
            pltpu.SemaphoreType.DMA((4,)),
            pltpu.SemaphoreType.DMA((per_group, groups, near)),
            pltpu.SemaphoreType.DMA((per_group, groups, near)),
            pltpu.SemaphoreType.DMA((near,)),
            pltpu.SemaphoreType.DMA((near,)),
            pltpu.SemaphoreType.DMA((per_group, far)),
            pltpu.SemaphoreType.DMA((per_group, far)),
            pltpu.SemaphoreType.DMA((per_group,)),
        ],
        compiler_params=pltpu.CompilerParams(
            collective_id=0, has_side_effects=True, vmem_limit_bytes=56 << 20
        ),
    )(sky_grad, kernel.T, owner_dev.transpose(0, 2, 1), cell_index, level_index)


def solution(mesh):
    near = 1 << (int(math.log2(mesh.shape["tile"])) // 2)
    return jax.shard_map(
        functools.partial(shards, near),
        mesh=mesh,
        in_specs=(
            P(None, ("tile", "shell"), None),
            P(),
            P("shell", "tile", None),
            P("shell", "tile"),
            P("shell", "tile"),
        ),
        out_specs=P("shell", "tile", None),
        check_vma=False,
    )
```

```python
import functools
import math

import jax
import jax.numpy as jnp
from jax import lax
from jax.experimental import pallas as pl
from jax.experimental.pallas import tpu as pltpu
from jax.sharding import PartitionSpec as P

LEVELS = 256
BLK_DEV = 256
RB = 16
EXT = BLK_DEV + RB
LANES = 128
MESH = pl.DeviceIdType.MESH


def body(
    groups, near, far,
    sky_hbm, kern, owner_hbm, cell_hbm, level_hbm, out,
    sky, owner, cell, level_in, index, red, rows, halves, part, landed, near_part, near_landed,
    load_sem, send_sem, recv_sem, far_send, far_recv, near_send, near_recv,
):
    bins, here, _ = sky.shape
    per_group = rows.shape[0]
    group = lax.axis_index("shell")
    tile = lax.axis_index("tile")
    hi = tile // near
    lo = tile % near

    low_half = hi < far // 2
    flipped = jnp.where(low_half, hi, far - 1 - hi)
    visits = []
    for h in range(max(1, far // 2)):
        visits.append(sorted((t for t in range(far) if t != h), key=lambda t: (-abs(t - h), t)) + [h])

    def visit(k):
        to = jnp.int32(0)
        for h, others in enumerate(visits):
            for n, t in enumerate(others):
                to = jnp.where((flipped == h) & (k == n), t, to)
        return jnp.where(low_half, to, far - 1 - to)

    def device(group_to, hi_to, lo_to):
        return {"shell": group_to, "tile": hi_to * near + lo_to}

    loads = [
        pltpu.make_async_copy(source, target, load_sem.at[n])
        for n, (source, target) in enumerate(
            [(sky_hbm, sky), (owner_hbm, owner), (cell_hbm, cell), (level_hbm, level_in)]
        )
    ]
    for load in loads:
        load.start()

    barrier = pltpu.get_barrier_semaphore()
    peers = [(d, e) for d in range(groups) for e in range(near) if (d, e) != (0, 0)]
    peers_of = [[(d, 0) for d in range(1, groups)]] * per_group
    for d, e in peers:
        pl.semaphore_signal(
            barrier, inc=1, device_id_type=MESH,
            device_id=device((group + d) % groups, hi, (lo + e) % near),
        )
    for f in range(1, far):
        pl.semaphore_signal(
            barrier, inc=1, device_id_type=MESH, device_id=device(group, (hi + f) % far, lo)
        )

    def row_copy(s, d, e):
        return pltpu.make_async_remote_copy(
            src_ref=red.at[s, d],
            dst_ref=rows.at[s, lo, pl.ds(pl.multiple_of(group * here, here), here)],
            send_sem=send_sem.at[s, d, e],
            recv_sem=recv_sem.at[s, d, e],
            device_id=device((group + d) % groups, hi, (lo + e) % near),
            device_id_type=MESH,
        )

    def near_copy(s, e, to):
        return pltpu.make_async_remote_copy(
            src_ref=near_part.at[s, e, to],
            dst_ref=near_landed.at[s, e, to],
            send_sem=near_send.at[s, e, to],
            recv_sem=near_recv.at[s, e, to],
            device_id=device(group, hi, (lo + e) % near),
            device_id_type=MESH,
        )

    def far_copy(s, to, slot):
        return pltpu.make_async_remote_copy(
            src_ref=part.at[s, to],
            dst_ref=landed.at[s, slot],
            send_sem=far_send.at[s, to],
            recv_sem=far_recv.at[s, slot],
            device_id=device(group, to, lo),
            device_id_type=MESH,
        )

    def reduce_bins(s, d):
        shell = ((group + d) % groups) * per_group + s
        total = kern[shell, 0] * sky[0]
        for b in range(1, bins):
            total = total + kern[shell, b] * sky[b]
        return total

    for load in loads[1:]:
        load.wait()
    for s in range(per_group):
        index[s : s + 1, :] = owner[s] * BLK_DEV + cell[s : s + 1, :]
        index[per_group + s : per_group + s + 1, :] = level_in[s : s + 1, :]
    loads[0].wait()
    order = sorted(range(groups), key=lambda d: (d == 0, abs(d - groups // 2)))
    for s in range(per_group):
        for n, d in enumerate(order):
            red[s, d] = reduce_bins(s, d)
            if s == 0 and n == 0:
                pl.semaphore_wait(barrier, len(peers) + far - 1)
            for e in reversed(range(near)):
                if (d, e) in peers_of[s]:
                    row_copy(s, d, e).start()
        rows[s, lo, pl.ds(pl.multiple_of(group * here, here), here)] = red[s, 0]

    def split(s, slot, n):
        whole = rows[s, n]
        top = whole.astype(jnp.bfloat16)
        halves[slot, :, :LANES] = top
        halves[slot, :, LANES:] = (whole - top.astype(jnp.float32)).astype(jnp.bfloat16)

    def deposit(s, indices, to, lo_to):
        first = (to * near + lo_to) * BLK_DEV - RB
        total = jnp.zeros((2 * EXT, 2 * LANES), jnp.float32)
        for slot, there in enumerate(indices):
            place = there[s : s + 1, :] - first
            level = there[per_group + s : per_group + s + 1, :].astype(jnp.float32)
            level = jnp.broadcast_to(level * (1.0 / LEVELS), (EXT, level.shape[1]))
            hit = lax.broadcasted_iota(jnp.int32, (EXT, place.shape[1]), 0) == place
            ones = jnp.where(hit, 1.0, 0.0).astype(jnp.bfloat16)
            levels = jnp.where(hit, level, 0.0).astype(jnp.bfloat16)
            total = total + jnp.dot(
                jnp.concatenate([ones, levels], axis=0), halves[slot],
                preferred_element_type=jnp.float32,
            )
        total = total[:, :LANES] + total[:, LANES:]
        landing = total[:EXT]
        shifted = total[EXT:] + landing * (0.5 / LEVELS)
        return landing[RB:] - shifted[RB:] + shifted[:BLK_DEV]

    def send_far(s, to):
        @pl.when(to != hi)
        def _():
            far_copy(s, to, hi).start()

    def near_sum(s, k):
        to = visit(k)
        for e in range(1, near):
            near_copy(s, e, to).wait_recv()
            part[s, to] += near_landed[s, e, to]
        send_far(s, to)

    def near_part_send(s):
        for d, e in peers_of[s]:
            row_copy(s, d, e).wait_recv()
        split(s, 0, lo)

        @pl.loop(0, far)
        def _(k):
            to = visit(k)
            for e in range(1, near):
                near_part[s, e, to] = deposit(s, [index], to, (lo + e) % near)
                near_copy(s, e, to).start()

    def own_part(s):
        @pl.loop(0, far)
        def _(k):
            to = visit(k)
            part[s, to] = deposit(s, [index], to, lo)

    for s in range(per_group):
        near_part_send(s)
        own_part(s)
        if s > 0:
            pl.loop(far // 2, far)(functools.partial(near_sum, s - 1))
        if s < per_group - 1:
            pl.loop(0, far // 2)(functools.partial(near_sum, s))
    pl.loop(0, far)(functools.partial(near_sum, per_group - 1))

    for s in range(per_group):
        out[s] = part[s, hi]
        for f in range(1, far):
            source = (hi + f) % far
            far_copy(s, source, source).wait_recv()
            out[s] += landed[s, source]

    for s in range(per_group):
        for d, e in peers_of[s]:
            row_copy(s, d, e).wait_send()
        for f in range(1, far):
            to = (hi + f) % far
            far_copy(s, to, to).wait_send()
    for e in range(1, near):
        for to in range(far):
            for s in range(per_group):
                near_copy(s, e, to).wait_send()


def shards(near, sky_grad, kernel, owner_dev, cell_index, level_index):
    groups, tiles = lax.axis_size("shell"), lax.axis_size("tile")
    far = tiles // near
    bins, here, lanes = sky_grad.shape
    per_group, tile_rows = cell_index.shape
    f32 = jnp.float32
    hbm = pl.BlockSpec(memory_space=pl.ANY)
    return pl.pallas_call(
        functools.partial(body, groups, near, far),
        out_shape=jax.ShapeDtypeStruct((per_group, BLK_DEV, lanes), f32),
        in_specs=[hbm, pl.BlockSpec(memory_space=pltpu.SMEM), hbm, hbm, hbm],
        out_specs=pl.BlockSpec(memory_space=pltpu.VMEM),
        scratch_shapes=[
            pltpu.VMEM((bins, here, lanes), f32),
            pltpu.VMEM((per_group, 1, tile_rows), jnp.int32),
            pltpu.VMEM((per_group, tile_rows), jnp.int32),
            pltpu.VMEM((per_group, tile_rows), jnp.int32),
            pltpu.VMEM((2 * per_group, tile_rows), jnp.int32),
            pltpu.VMEM((per_group, groups, here, lanes), f32),
            pltpu.VMEM((per_group, near, tile_rows, lanes), f32),
            pltpu.VMEM((near, tile_rows, 2 * lanes), jnp.bfloat16),
            pltpu.VMEM((per_group, far, BLK_DEV, lanes), f32),
            pltpu.VMEM((per_group, far, BLK_DEV, lanes), f32),
            pltpu.VMEM((per_group, near, far, BLK_DEV, lanes), f32),
            pltpu.VMEM((per_group, near, far, BLK_DEV, lanes), f32),
            pltpu.SemaphoreType.DMA((4,)),
            pltpu.SemaphoreType.DMA((per_group, groups, near)),
            pltpu.SemaphoreType.DMA((per_group, groups, near)),
            pltpu.SemaphoreType.DMA((per_group, far)),
            pltpu.SemaphoreType.DMA((per_group, far)),
            pltpu.SemaphoreType.DMA((per_group, near, far)),
            pltpu.SemaphoreType.DMA((per_group, near, far)),
        ],
        compiler_params=pltpu.CompilerParams(
            collective_id=0, has_side_effects=True, vmem_limit_bytes=56 << 20
        ),
    )(sky_grad, kernel.T, owner_dev.transpose(0, 2, 1), cell_index, level_index)


def solution(mesh):
    near = 1 << (int(math.log2(mesh.shape["tile"])) // 2)
    return jax.shard_map(
        functools.partial(shards, near),
        mesh=mesh,
        in_specs=(
            P(None, ("tile", "shell"), None),
            P(),
            P("shell", "tile", None),
            P("shell", "tile"),
            P("shell", "tile"),
        ),
        out_specs=P("shell", "tile", None),
        check_vma=False,
    )
```
